768 devices in a mesh: member: 48 (over y_lo, z, core), domain: 16 (over x, y_hi).
Axes of the slice: x: 4, y: 8 (y_hi: 4, y_lo: 2; y = y_hi * 2 + y_lo), z: 12, core: 2. Of those that a mesh axis runs over, the one named last changes fastest.
Arguments:
- perturb: bfloat16 [192, 1536, 2048], P('member', None, 'domain'), may hold values from -20 to 20
- courant: float32 [2, 1536, 2048], P(None, 'member', 'domain'), may hold values from -0.45 to 0.45
- land_sea: int32 [1536, 2048], P('member', 'domain'), may hold values from 0 to 1, as said below
- basin_labels: int32 [96], replicated, may hold values from 0 to 3
- row_depth: float32 [1536], replicated, may hold values from 50 to 5000
- sample_column: int32 [3, 1536, 256], P(None, 'member', 'domain'), may hold values from 0 to 2047, as said below
- innovation: float32 [3, 1536, 256], P(None, 'member', 'domain'), may hold values from -6 to 6
- error_weight: float32 [3, 1536, 256], P(None, 'member', 'domain'), may hold values from 0.25 to 4
Outputs:
- increment: float32 [1536, 2048], P('member', 'domain')
- equivalents: float32 [3, 1536, 256], P(None, 'member', 'domain')
The draws below stay inside these ranges and needn't reach their ends.
Inputs may be any that keep to these rules, and one draw needn't show every extreme that they name: `land_sea`: 0 marks land and 1 sea; rows 0 and 1535 are land. `sample_column`: entry j of a row lies in domain tile j // 16: 128 * (j // 16) <= value < 128 * (j // 16 + 1); columns may repeat.
All inputs are finite; a program needn't handle non-finite values.
Results may differ from the reference program's by a relative error of at most 0.0047.
Values may be sent and summed in bfloat16 or wider, within the bound.
A program may use at most 64 MiB of HBM per device.

```python
import math
import jax
import jax.numpy as jnp
from jax import lax

DX = 128
NSTEP = 3
ITERS = 2
OBS_TILE = 16
LOC_ROWS = 16
NGROUP = 4
K = 192
NY = 1536
NX = 2048
NOBS = 256
NBLK = 96


def draw_perturb(key, part):
    base_key, column_key, member_key = jax.random.split(key, 3)
    row_fraction = jnp.arange(NY, dtype=jnp.float32) / (NY - 1)
    row_scale = jnp.exp(0.5 * jnp.log(3.0) * row_fraction)
    column_scale = jnp.exp(jax.random.uniform(column_key, (NX,), minval=0.0, maxval=0.5 * jnp.log(3.0)))
    member_scale = jnp.exp(jax.random.uniform(member_key, (K,), minval=-0.5, maxval=0.5))
    entries = jax.random.normal(base_key, (K, NY, NX))
    entries = jnp.clip(entries, -4.0, 4.0)
    scaled = entries * member_scale[:, None, None] * row_scale[None, :, None] * column_scale[None, None, :]
    return scaled.astype(jnp.float32).astype(jnp.bfloat16)


def draw_land_sea(key, part):
    uniform_draw = jax.random.randint(key, (NY, NX), 0, 5)
    is_sea = jnp.where(uniform_draw > 0, 1, 0)
    row_index = lax.broadcasted_iota(jnp.int32, (NY, NX), 0)
    interior = (row_index > 0) & (row_index < NY - 1)
    return jnp.where(interior, is_sea, 0).astype(jnp.int32)


def draw_sample_column(key, part):
    local_column = jax.random.randint(key, (NSTEP, NY, NOBS), 0, DX)
    slot_index = lax.broadcasted_iota(jnp.int32, (NSTEP, NY, NOBS), 2)
    row_index = lax.broadcasted_iota(jnp.int32, (NSTEP, NY, NOBS), 1)
    step_index = lax.broadcasted_iota(jnp.int32, (NSTEP, NY, NOBS), 0)
    first_row_mask = (row_index == 0) & (step_index == 0)
    local_column = jnp.where(first_row_mask & (slot_index % OBS_TILE == 0), 0, local_column)
    local_column = jnp.where(first_row_mask & (slot_index % OBS_TILE == OBS_TILE - 1), DX - 1, local_column)
    return (local_column + slot_index // OBS_TILE * DX).astype(jnp.int32)


def touch_ends(array, rng, least, high):
    longest = array.shape.index(max(array.shape))
    spots = []
    for shift in (0, 1):
        where = [jax.random.randint(jax.random.fold_in(rng, axis), (), 0, length) for axis, length in enumerate(array.shape)]
        where[longest] = (where[longest] + shift) % array.shape[longest]
        spots.append(tuple(where))
    return array.at[spots[0]].set(least).at[spots[1]].set(high)


def steps_of(rng, shape, cuts, low, largest):
    gain, own = 1.0, jax.random.fold_in(rng, 6)
    for axis_at, shards_of in cuts:
        heights = jnp.exp(jax.random.uniform(jax.random.fold_in(own, axis_at), (shards_of,), jnp.float32, low / len(cuts), largest / len(cuts)))
        gain = gain * jnp.repeat(heights, shape[axis_at] // shards_of).reshape([-1 if axis == axis_at else 1 for axis in range(len(shape))])
    return gain


def scatter_about(key, extent, deviation, most, cuts=(), kind=jnp.bfloat16):
    array = jax.random.normal(key, extent, jnp.float32) * deviation
    if len(cuts) > 0:
        array = steps_of(key, extent, cuts, -0.22, 0.18) * array
    return jnp.clip(array, min=-most, max=most).astype(kind)


def setup_inputs(seed: int = 0) -> dict:
    key_of = jax.random.split(jax.random.key(seed), 9)
    return {
        "perturb": draw_perturb(jax.random.fold_in(key_of[8], 71), 0),
        "courant": jnp.clip(jax.random.uniform(key_of[1], (2, NY, NX), jnp.float32, -0.45, 0.45) * steps_of(key_of[1], (2, NY, NX), ((1, 48), (2, 16)), -0.4, 0.0), -0.45, 0.45),
        "land_sea": draw_land_sea(jax.random.fold_in(key_of[8], 71), 0),
        "basin_labels": touch_ends(jax.random.randint(key_of[3], (NBLK,), 0, NGROUP), jax.random.fold_in(key_of[3], 1), 0, NGROUP - 1).astype(jnp.int32),
        "row_depth": jnp.clip(jnp.exp(jax.random.uniform(key_of[4], (NY,), jnp.float32, math.log(50.0), math.log(5000.0))), 50.0, 5000.0),
        "sample_column": draw_sample_column(jax.random.fold_in(key_of[8], 71), 0),
        "innovation": scatter_about(key_of[6], (NSTEP, NY, NOBS), 1.0, 6.0, ((1, 48), (2, 16)), jnp.float32),
        "error_weight": jnp.clip(jnp.exp(math.log(4.0) - 2.7725887 * jax.random.uniform(key_of[7], (NSTEP, NY, NOBS), jnp.float32) ** steps_of(key_of[7], (NSTEP, NY, NOBS), ((1, 48), (2, 16)), -0.2, 0.2)), 0.25, 4.0),
    }


def localization(basin_labels, row_depth):
    row_index = jnp.arange(NY, dtype=jnp.int32)
    spacing = jnp.abs(row_index[:, None] - row_index[None, :])
    distance = jnp.minimum(spacing, NY - spacing).astype(jnp.float32)
    kernel = jnp.cosh(2.0 - 4.0 * distance / NY) / jnp.cosh(jnp.float32(2.0))
    labels = jnp.repeat(basin_labels, LOC_ROWS)
    matched = (labels[:, None] == labels[None, :]).astype(jnp.float32)
    log_depth = jnp.log(row_depth)
    depth_factor = jnp.exp(-jnp.abs(log_depth[:, None] - log_depth[None, :]))
    return (kernel * (1.0 + matched) * depth_factor).astype(jnp.bfloat16)


def covariance(vector, perturb, sea_mask, localizer):
    shared = (sea_mask * vector).astype(jnp.bfloat16)

    def add_member(running, member):
        weighted = (member.astype(jnp.float32) * shared.astype(jnp.float32)).astype(jnp.bfloat16)
        spread = jnp.dot(localizer, weighted, preferred_element_type=jnp.float32)
        return running + member.astype(jnp.float32) * spread, None

    running, _ = lax.scan(add_member, jnp.zeros((NY, NX), jnp.float32), perturb)
    return sea_mask * running / (K - 1)


def advance(state_field, courant, sea_mask):
    eastward = jnp.maximum(courant[0], 0.0)
    westward = jnp.maximum(-courant[0], 0.0)
    northward = jnp.maximum(courant[1], 0.0)
    southward = jnp.maximum(-courant[1], 0.0)
    retain = 1.0 - jnp.abs(courant[0]) - jnp.abs(courant[1])
    advected = retain * state_field + eastward * jnp.roll(state_field, 1, 1) + westward * jnp.roll(state_field, -1, 1)
    advected = advected + northward * jnp.roll(state_field, 1, 0) + southward * jnp.roll(state_field, -1, 0)
    return sea_mask * advected


def retreat(adjoint_field, courant, sea_mask):
    eastward = jnp.maximum(courant[0], 0.0)
    westward = jnp.maximum(-courant[0], 0.0)
    northward = jnp.maximum(courant[1], 0.0)
    southward = jnp.maximum(-courant[1], 0.0)
    retain = 1.0 - jnp.abs(courant[0]) - jnp.abs(courant[1])
    masked = sea_mask * adjoint_field
    result = retain * masked + jnp.roll(eastward * masked, -1, 1) + jnp.roll(westward * masked, 1, 1)
    result = result + jnp.roll(northward * masked, -1, 0) + jnp.roll(southward * masked, 1, 0)
    return result


def reference(perturb, courant, land_sea, basin_labels, row_depth, sample_column, innovation, error_weight):
    sea_mask = land_sea.astype(jnp.float32)
    localizer = localization(basin_labels, row_depth)
    row_index = lax.broadcasted_iota(jnp.int32, (NY, NOBS), 0)

    def tangent(vector):
        state_field = vector
        observed = []
        for moment in range(NSTEP):
            state_field = advance(state_field, courant, sea_mask)
            observed.append(jnp.take_along_axis(state_field, sample_column[moment], axis=1))
        return jnp.stack(observed)

    def adjoint(forcing):
        state_field = jnp.zeros((NY, NX), jnp.float32)
        for moment in reversed(range(NSTEP)):
            state_field = state_field.at[row_index, sample_column[moment]].add(forcing[moment])
            state_field = retreat(state_field, courant, sea_mask)
        return state_field

    increment = jnp.zeros((NY, NX), jnp.float32)
    control = jnp.zeros((NY, NX), jnp.float32)
    equivalents = jnp.zeros((NSTEP, NY, NOBS), jnp.float32)
    for iteration in range(ITERS):
        forcing = error_weight * (equivalents - innovation)
        adjoint_grad = adjoint(forcing)
        gradient = control + adjoint_grad
        direction = increment + covariance(adjoint_grad, perturb, sea_mask, localizer)
        curvature = jnp.sum(gradient * direction)
        observed = tangent(direction)
        misfit = jnp.sum(error_weight * observed * observed)
        step_size = curvature / (curvature + misfit)
        increment = increment - step_size * direction
        control = control - step_size * gradient
        equivalents = equivalents - step_size * observed
    return increment, equivalents
```

```python
import functools
import math

import jax
import jax.numpy as jnp
from jax import lax
from jax.experimental import pallas as pl
from jax.experimental.pallas import tpu as pltpu
from jax.sharding import PartitionSpec as P

NSTEP = 3
LOC_ROWS = 16
FIELDS = 9
EDGE = 8
SCALE = 2.0**-10
MESH = pl.DeviceIdType.MESH
F32 = jnp.float32
BF16 = jnp.bfloat16
AROUND = [(dm, dd) for dm in (-1, 0, 1) for dd in (-1, 0, 1) if (dm, dd) != (0, 0)]


def kernel(
    ensemble,
    pert_hbm,
    courant,
    land_sea,
    label_scalars,
    label_vector,
    depth_row,
    sample_column,
    innovation,
    error_weight,
    increment_out,
    equivalents_out,
    pert,
    loc,
    weighted,
    spread,
    base,
    depth_col,
    fields,
    pack_out,
    pack_in,
    coef,
    weight_ext,
    force_ext,
    whole,
    rs_send,
    rs_recv,
    grad,
    tile,
    seen,
    col_pad,
    ar_send,
    ar_a,
    ar_b,
    local_sem,
    pert_sems,
    rim_send,
    rim_recv,
    gat_send,
    gat_recv,
    fwd_send,
    fwd_recv,
    red_send,
    red_recv,
    ara_send,
    ara_recv,
    arb_send,
    arb_recv,
):
    count_m = lax.axis_size("member")
    count_d = lax.axis_size("domain")
    m = lax.axis_index("member")
    d = lax.axis_index("domain")
    peers = count_m // 2
    deep = peers // 2
    total = 32 * count_m
    tiles = total // 128
    core = lax.rem(m, 2)
    p = m // 2
    half = p // deep
    z = lax.rem(p, deep)
    sibling = {"member": 2 * p + 1 - core, "domain": d}

    def place_to(s):
        return lax.rem(half + lax.rem(s, 2), 2) * deep + lax.rem(z + s // 2, deep)

    def place_from(s):
        return lax.rem(half + lax.rem(s, 2), 2) * deep + lax.rem(z - s // 2 + deep, deep)

    def peer(s):
        return {"member": 2 * place_to(s) + core, "domain": d}

    def crossing(q):
        return {
            "member": 2 * p + lax.rem(core + lax.rem(q, 2), 2),
            "domain": lax.rem(d + q // 2, count_d),
        }

    def around(dm, dd):
        return {
            "member": lax.rem(m + dm + count_m, count_m),
            "domain": lax.rem(d + dd + count_d, count_d),
        }

    def remote(src, dst, send, recv, device):
        return pltpu.make_async_remote_copy(
            src_ref=src, dst_ref=dst, send_sem=send, recv_sem=recv, device_id=device, device_id_type=MESH
        )

    load = pltpu.make_async_copy(pert_hbm, pert.at[pl.ds(0, 4)], local_sem)
    load.start()

    barrier = pltpu.get_barrier_semaphore()

    def greet_peer(s, carry):
        pl.semaphore_signal(barrier, inc=1, device_id=peer(s), device_id_type=MESH)
        return carry

    def greet_crossing(q, carry):
        pl.semaphore_signal(barrier, inc=1, device_id=crossing(q), device_id_type=MESH)
        return carry

    for dm, dd in AROUND:
        pl.semaphore_signal(barrier, inc=1, device_id=around(dm, dd), device_id_type=MESH)
    lax.fori_loop(1, peers, greet_peer, 0)
    lax.fori_loop(1, 2 * count_d, greet_crossing, 0)

    lane = lax.broadcasted_iota(jnp.int32, (32, 128), 1)
    sea = land_sea[...].astype(F32)
    fields[0, 0:32, :] = courant[0]
    fields[1, 0:32, :] = courant[1]
    fields[2, 0:32, :] = sea
    for t in range(NSTEP):
        column = sample_column[t] - d * 128
        col_pad[t] = jnp.zeros((32, 128), jnp.int32)
        col_pad[t, :, 0:16] = column
        ew = error_weight[t]
        push = -ew * innovation[t]
        w_sum = jnp.zeros((32, 128), F32)
        g_sum = jnp.zeros((32, 128), F32)
        for j in range(16):
            hit = column[:, j : j + 1] == lane
            w_sum = w_sum + jnp.where(hit, ew[:, j : j + 1], 0.0)
            g_sum = g_sum + jnp.where(hit, push[:, j : j + 1], 0.0)
        fields[3 + t, 0:32, :] = w_sum
        fields[6 + t, 0:32, :] = g_sum
    first = jnp.zeros((32, 128), F32)
    last = jnp.zeros((32, 128), F32)
    for f in range(FIELDS):
        here = (lane >= EDGE * f) & (lane < EDGE * (f + 1))
        value = fields[f, 0:32, :]
        turned = value if f == 0 else pltpu.roll(value, EDGE * f, 1)
        first = jnp.where(here, turned, first)
        last = jnp.where(here, pltpu.roll(value, EDGE * (f + 1), 1), last)
    pack_out[0] = first
    pack_out[1] = last

    pl.semaphore_wait(barrier, 8 + (peers - 1) + (2 * count_d - 1))

    def rows_of(dm):
        if dm == 0:
            return slice(0, 32), slice(0, 32)
        if dm == 1:
            return slice(24, 32), slice(40, 48)
        return slice(0, 8), slice(32, 40)

    def rim_copy(n, i):
        dm, dd = AROUND[i]
        src, dst = rows_of(dm)
        if n == 0:
            if dd == 0:
                a, b = fields.at[:, src, :], fields.at[:, dst, :]
            else:
                side = 0 if dd < 0 else 1
                a, b = pack_out.at[side, src, :], pack_in.at[side, dst, :]
        else:
            a = tile.at[n - 1, 0, src, :]
            b = tile.at[n - 1, 0 if dd == 0 else (1 if dd < 0 else 2), dst, :]
        return remote(a, b, rim_send.at[n, i], rim_recv.at[n, i], around(dm, dd))

    for i in range(8):
        rim_copy(0, i).start()
    share = remote(pert_hbm, pert.at[pl.ds(4, 4)], pert_sems.at[0], pert_sems.at[1], sibling)
    share.start()

    row_i = lax.broadcasted_iota(jnp.int32, (128, 128), 0)
    lane_i = lax.broadcasted_iota(jnp.int32, (128, 128), 1)
    for t in range(tiles):
        gap = jnp.abs(lane_i + 128 * t - row_i)
        gap = jnp.minimum(gap, total - gap).astype(F32)
        x = 2.0 - 4.0 * gap / total
        value = (jnp.exp(x) + jnp.exp(-x)) / (2.0 * math.cosh(2.0))
        base[:, 128 * t : 128 * (t + 1)] = value
        base[:, total + 128 * t : total + 128 * (t + 1)] = value
        row = jnp.broadcast_to(depth_row[:, 128 * t : 128 * (t + 1)], (128, 128))
        turned = row.T
        depth_col[0, 128 * t : 128 * (t + 1), :] = turned
        depth_col[1, 128 * t : 128 * (t + 1), :] = 1.0 / turned
    blocks = total // LOC_ROWS
    spot = lax.broadcasted_iota(jnp.int32, (blocks, total), 1) // LOC_ROWS
    own_block = lax.broadcasted_iota(jnp.int32, (blocks, total), 0)
    labels = jnp.dot(
        jnp.broadcast_to(label_vector[...].astype(F32), (8, blocks)),
        (spot == own_block).astype(F32),
        preferred_element_type=F32,
    )[0:1, :]
    depth = depth_row[...]
    depth_inv = 1.0 / depth

    def localize(s, carry):
        q = place_to(s)
        for h in range(2):
            label = label_scalars[4 * q + 2 * core + h].astype(F32)
            factor = jnp.where(jnp.abs(labels - label) < 0.5, 2.0, 1.0)
            near = depth * factor
            near_inv = depth_inv * factor
            rows = pl.ds(pl.multiple_of(64 * q + 32 * core + 16 * h, 16), 16)
            base_rows = pl.ds(pl.multiple_of(64 * lax.rem(q, 2) + 32 * core + 16 * h, 16), 16)
            a = depth_col[0, rows, :]
            a_inv = depth_col[1, rows, :]
            out_rows = pl.ds(pl.multiple_of(32 * s + 16 * h, 16), 16)
            for t in range(tiles):
                cols = slice(128 * t, 128 * (t + 1))
                ratio = jnp.minimum(a * near_inv[:, cols], a_inv * near[:, cols])
                offset = pl.multiple_of(128 * (tiles - q // 2 + t), 128)
                loc[out_rows, cols] = (ratio * base[base_rows, pl.ds(offset, 128)]).astype(BF16)
        return carry

    split = peers // 2
    lax.fori_loop(0, split, localize, 0)

    for i in range(8):
        rim_copy(0, i).wait()

    lane48 = lax.broadcasted_iota(jnp.int32, (48, 128), 1)
    ext = []
    for f in range(FIELDS):
        right = pack_in[0] if f == 0 else pltpu.roll(pack_in[0], 128 - EDGE * f, 1)
        left = pltpu.roll(pack_in[1], 128 - EDGE * (f + 1), 1)
        ext.append(jnp.concatenate([fields[f], jnp.where(lane48 < 64, right, left)], axis=1))
    cu, cv, sea_ext = ext[0], ext[1], ext[2]
    coef[0] = 1.0 - jnp.abs(cu) - jnp.abs(cv)
    coef[1] = jnp.maximum(cu, 0.0)
    coef[2] = jnp.maximum(-cu, 0.0)
    coef[3] = jnp.maximum(cv, 0.0)
    coef[4] = jnp.maximum(-cv, 0.0)
    coef[5] = sea_ext
    for t in range(NSTEP):
        weight_ext[t] = ext[3 + t]
        force_ext[t] = ext[6 + t]

    def shift(value, by, axis):
        return pltpu.roll(value, by % value.shape[axis], axis)

    def advance(s):
        moved = coef[0] * s + coef[1] * shift(s, 1, 1) + coef[2] * shift(s, -1, 1)
        moved = moved + coef[3] * shift(s, 1, 0) + coef[4] * shift(s, -1, 0)
        return coef[5] * moved

    def retreat(adj):
        masked = coef[5] * adj
        back = coef[0] * masked + shift(coef[1] * masked, -1, 1) + shift(coef[2] * masked, 1, 1)
        return back + shift(coef[3] * masked, -1, 0) + shift(coef[4] * masked, 1, 0)

    def adjoint(forces):
        adj = retreat(forces[2])
        adj = retreat(adj + forces[1])
        return retreat(adj + forces[0])[0:32, 0:128]

    def scatter_gather(n):
        whole[n, p, core] = (sea * grad[n]).astype(BF16)

        def gather_copy(s, where):
            return remote(
                whole.at[n, where, core],
                whole.at[n, where, core],
                gat_send.at[n, s],
                gat_recv.at[n, s],
                peer(s),
            )

        def forward_copy(s, side):
            q = place_from(s)
            return remote(
                whole.at[n, q, side], whole.at[n, q, side], fwd_send.at[n, s], fwd_recv.at[n, s], sibling
            )

        def send(s, carry):
            gather_copy(s, p).start()
            return carry

        forward_copy(0, core).start()
        lax.fori_loop(1, peers, send, 0)
        if n == 0:
            lax.fori_loop(split, peers, localize, 0)
            load.wait()
            share.wait()

        def weigh(q, side):
            rows = pl.ds(pl.multiple_of(64 * q + 32 * side, 32), 32)
            v = whole[n, q, side]
            for k in range(8):
                weighted[rows, 128 * k : 128 * (k + 1)] = pert[k, rows, :] * v

        def arrive(s, carry):
            gather_copy(s, place_from(s)).wait_recv()
            forward_copy(s, core).start()
            weigh(place_from(s), core)
            return carry

        def arrive_forward(s, carry):
            forward_copy(s, 1 - core).wait_recv()
            weigh(place_from(s), 1 - core)
            return carry

        weigh(p, core)
        lax.fori_loop(1, peers, arrive, 0)
        lax.fori_loop(0, peers, arrive_forward, 0)

        def reduce_copy(s):
            return remote(
                rs_send.at[n, s], rs_recv.at[n, s], red_send.at[n, s], red_recv.at[n, s], peer(s)
            )

        chunks = 3 if peers % 3 == 0 else 2
        slots = peers // chunks

        def share_of(s, i):
            rows = pl.ds(pl.multiple_of(64 * place_to(s) + 32 * core, 32), 32)
            rows_in = pl.ds(pl.multiple_of(32 * i, 32), 32)
            acc = pert[0, rows, :].astype(F32) * spread[rows_in, 0:128]
            for k in range(1, 8):
                acc = acc + pert[k, rows, :].astype(F32) * spread[rows_in, 128 * k : 128 * (k + 1)]
            return acc

        def chunk(step, carry):
            ci = lax.rem(step + 1, chunks)
            first_row = pl.multiple_of(ci * slots * 32, 32)
            spread[...] = jnp.dot(
                loc[pl.ds(first_row, slots * 32), :], weighted[...], preferred_element_type=F32
            )

            def out(i, inner):
                s = ci * slots + i

                @pl.when(s > 0)
                def _():
                    rs_send[n, s] = share_of(s, i).astype(BF16)
                    reduce_copy(s).start()

                return inner

            lax.fori_loop(0, slots, out, 0)
            return carry

        lax.fori_loop(0, chunks, chunk, 0)
        acc = share_of(0, 0)

        def collect(s, acc):
            reduce_copy(s).wait_recv()
            return acc + rs_recv[n, s].astype(F32)

        acc = lax.fori_loop(1, peers, collect, acc)
        tile[n, 0, 0:32, :] = sea * acc / (ensemble - 1)
        for i in range(8):
            rim_copy(n + 1, i).start()

    def finish_sends(n):
        def body(s, carry):
            remote(
                whole.at[n, p, core], whole.at[n, p, core], gat_send.at[n, s], gat_recv.at[n, s], peer(s)
            ).wait_send()
            remote(
                rs_send.at[n, s], rs_recv.at[n, s], red_send.at[n, s], red_recv.at[n, s], peer(s)
            ).wait_send()
            return carry

        def body_forward(s, carry):
            q = place_from(s)
            remote(
                whole.at[n, q, core], whole.at[n, q, core], fwd_send.at[n, s], fwd_recv.at[n, s], sibling
            ).wait_send()
            return carry

        lax.fori_loop(1, peers, body, 0)
        lax.fori_loop(0, peers, body_forward, 0)

    def widened(n):
        for i in range(8):
            rim_copy(n + 1, i).wait()
        side = jnp.where(lane48 < 64, tile[n, 1], tile[n, 2])
        return jnp.concatenate([tile[n, 0], side], axis=1)

    def tangent(s):
        states = []
        for t in range(NSTEP):
            s = advance(s)
            states.append(s)
        return states

    def sample(states, n):
        for t in range(NSTEP):
            seen[n, t] = jnp.take_along_axis(states[t][0:32, 0:128], col_pad[t], axis=1)

    def added(value):
        return jnp.sum(jnp.sum(value, axis=0, keepdims=True), axis=1, keepdims=True)

    def inner(x):
        return x[0:32, 0:128]

    grad[0] = adjoint([force_ext[t] for t in range(NSTEP)])
    scatter_gather(0)
    first_states = tangent(widened(0))
    pulls = [weight_ext[t] * first_states[t] for t in range(NSTEP)]
    grad[1] = adjoint(pulls) * SCALE
    for t in range(NSTEP):
        force_ext[t] = pulls[t]
    first_own = first_states
    sample(first_states, 0)
    misfit_11 = added(sum(inner(pulls[t]) * inner(first_own[t]) for t in range(NSTEP)))
    scatter_gather(1)
    finish_sends(0)
    d1 = tile[0, 0, 0:32, :]
    d2 = tile[1, 0, 0:32, :]
    curve_11 = added(grad[0] * d1)
    curve_12 = added(grad[0] * d2 + grad[1] * d1)
    curve_22 = added(grad[1] * d2)
    second_states = tangent(widened(1))
    misfit_12 = added(sum(inner(force_ext[t]) * inner(second_states[t]) for t in range(NSTEP)))
    misfit_22 = added(
        sum(inner(weight_ext[t]) * inner(second_states[t]) * inner(second_states[t]) for t in range(NSTEP))
    )

    lane1 = lax.broadcasted_iota(jnp.int32, (1, 128), 1)
    sums = jnp.zeros((1, 128), F32)
    for i, value in enumerate((curve_11, curve_12, curve_22, misfit_11, misfit_12, misfit_22)):
        sums = jnp.where(lane1 == i, value, sums)

    def ar_copy(stage, s):
        if stage == 0:
            return remote(ar_send.at[0], ar_a.at[s], ara_send.at[s], ara_recv.at[s], peer(s))
        return remote(ar_send.at[1], ar_b.at[s], arb_send.at[s], arb_recv.at[s], crossing(s))

    for stage, slots in ((0, peers), (1, 2 * count_d)):
        ar_send[stage] = sums

        def start(s, carry):
            ar_copy(stage, s).start()
            return carry

        def gain(s, acc):
            ar_copy(stage, s).wait_recv()
            return acc + (ar_a[s] if stage == 0 else ar_b[s])

        lax.fori_loop(1, slots, start, 0)
        if stage == 0:
            sample(second_states, 1)
            finish_sends(1)
        sums = lax.fori_loop(1, slots, gain, sums)

    def total_of(i):
        return jnp.sum(jnp.where(lane1 == i, sums, 0.0), axis=1, keepdims=True)

    curve_11, curve_12, curve_22 = total_of(0), total_of(1), total_of(2)
    misfit_11, misfit_12, misfit_22 = total_of(3), total_of(4), total_of(5)
    step_1 = curve_11 / (curve_11 + misfit_11)
    keep = 1.0 - step_1
    mix = step_1 * (1.0 / SCALE)
    curve = keep * keep * curve_11 - mix * keep * curve_12 + mix * mix * curve_22
    misfit = keep * keep * misfit_11 - 2.0 * mix * keep * misfit_12 + mix * mix * misfit_22
    step_2 = curve / (curve + misfit)
    a = -step_1 - step_2 * keep
    b = step_2 * mix
    increment_out[...] = a * d1 + b * d2
    for t in range(NSTEP):
        equivalents_out[t] = (a * seen[0, t] + b * seen[1, t])[:, 0:16]

    def end(stage):
        def body(s, carry):
            ar_copy(stage, s).wait_send()
            return carry

        return body

    lax.fori_loop(1, peers, end(0), 0)
    lax.fori_loop(1, 2 * count_d, end(1), 0)


def per_device(
    perturb, courant, land_sea, basin_labels, row_depth, sample_column, innovation, error_weight
):
    members, total, width = perturb.shape
    rows = land_sea.shape[0]
    count_m = lax.axis_size("member")
    count_d = lax.axis_size("domain")
    peers = count_m // 2
    chunks = 3 if peers % 3 == 0 else 2
    vmem = pl.BlockSpec(memory_space=pltpu.VMEM)
    dma = pltpu.SemaphoreType.DMA
    return pl.pallas_call(
        functools.partial(kernel, members * count_m),
        out_shape=(
            jax.ShapeDtypeStruct((rows, width), F32),
            jax.ShapeDtypeStruct(innovation.shape, F32),
        ),
        in_specs=[
            pl.BlockSpec(memory_space=pl.ANY),
            vmem,
            vmem,
            pl.BlockSpec(memory_space=pltpu.SMEM),
            vmem,
            vmem,
            vmem,
            vmem,
            vmem,
        ],
        out_specs=(vmem, vmem),
        scratch_shapes=[
            pltpu.VMEM((2 * members, total, width), BF16),
            pltpu.VMEM((total // 2, total), BF16),
            pltpu.VMEM((total, 2 * members * width), BF16),
            pltpu.VMEM((total // 2 // chunks, 2 * members * width), F32),
            pltpu.VMEM((128, 2 * total), F32),
            pltpu.VMEM((2, total, 128), F32),
            pltpu.VMEM((FIELDS, 48, 128), F32),
            pltpu.VMEM((2, 32, 128), F32),
            pltpu.VMEM((2, 48, 128), F32),
            pltpu.VMEM((6, 48, 256), F32),
            pltpu.VMEM((NSTEP, 48, 256), F32),
            pltpu.VMEM((NSTEP, 48, 256), F32),
            pltpu.VMEM((2, peers, 2, 32, 128), BF16),
            pltpu.VMEM((2, peers, 32, 128), BF16),
            pltpu.VMEM((2, peers, 32, 128), BF16),
            pltpu.VMEM((2, 32, 128), F32),
            pltpu.VMEM((2, 3, 48, 128), F32),
            pltpu.VMEM((2, NSTEP, 32, 128), F32),
            pltpu.VMEM((NSTEP, 32, 128), jnp.int32),
            pltpu.VMEM((2, 1, 128), F32),
            pltpu.VMEM((peers, 1, 128), F32),
            pltpu.VMEM((2 * count_d, 1, 128), F32),
            dma,
            dma((2,)),
            dma((3, 8)),
            dma((3, 8)),
            dma((2, peers)),
            dma((2, peers)),
            dma((2, peers)),
            dma((2, peers)),
            dma((2, peers)),
            dma((2, peers)),
            dma((peers,)),
            dma((peers,)),
            dma((2 * count_d,)),
            dma((2 * count_d,)),
        ],
        compiler_params=pltpu.CompilerParams(
            collective_id=0, has_side_effects=True, vmem_limit_bytes=48 * 1024 * 1024
        ),
    )(
        perturb,
        courant,
        land_sea,
        basin_labels,
        basin_labels.reshape(1, -1),
        row_depth.reshape(1, -1),
        sample_column,
        innovation,
        error_weight,
    )


def solution(mesh):
    in_specs = (
        P("member", None, "domain"),
        P(None, "member", "domain"),
        P("member", "domain"),
        P(),
        P(),
        P(None, "member", "domain"),
        P(None, "member", "domain"),
        P(None, "member", "domain"),
    )
    out_specs = (P("member", "domain"), P(None, "member", "domain"))
    return jax.shard_map(
        per_device, mesh=mesh, in_specs=in_specs, out_specs=out_specs, check_vma=False
    )
```

```python
import functools
import math

import jax
import jax.numpy as jnp
from jax import lax
from jax.experimental import pallas as pl
from jax.experimental.pallas import tpu as pltpu
from jax.sharding import PartitionSpec as P

NSTEP = 3
LOC_ROWS = 16
FIELDS = 9
CHUNKS = 4
EDGE = 8
SCALE = 2.0**-10
MESH = pl.DeviceIdType.MESH
F32 = jnp.float32
BF16 = jnp.bfloat16
AROUND = [(dm, dd) for dm in (-1, 0, 1) for dd in (-1, 0, 1) if (dm, dd) != (0, 0)]


def kernel(
    ensemble,
    pert_hbm,
    courant_hbm,
    sea_hbm,
    label_hbm,
    depth_hbm,
    column_hbm,
    innovation_hbm,
    weight_hbm,
    increment_out,
    equivalents_out,
    pert,
    loc,
    weighted,
    spread,
    base,
    depth_col,
    depth_row,
    label_scalars,
    label_vector,
    land_sea,
    obs_int,
    obs_real,
    turn,
    fields,
    pack_out,
    pack_in,
    coef,
    weight_ext,
    force_ext,
    whole,
    rs_send,
    rs_recv,
    grad,
    tile,
    seen,
    pick,
    ar_send,
    ar_a,
    ar_b,
    local_sems,
    pert_sems,
    rim_send,
    rim_recv,
    gat_send,
    gat_recv,
    fwd_recv,
    red_send,
    red_recv,
    ar_send_sem,
    ar_recv_sem,
):
    count_m = lax.axis_size("member")
    count_d = lax.axis_size("domain")
    m = lax.axis_index("member")
    d = lax.axis_index("domain")
    peers = count_m // 2
    deep = peers // 2
    total = 32 * count_m
    tiles = total // 128
    core = lax.rem(m, 2)
    p = m // 2
    half = p // deep
    z = lax.rem(p, deep)
    sibling = {"member": 2 * p + 1 - core, "domain": d}

    near = min(2, deep // 6)
    low, high = near + 1, deep - near
    third = (high - low) // 3
    groups = [(low + third, high - third), (low, low + third), (high - third, high)]
    groups = [group for group in groups if group[0] < group[1]]

    def plane(dy):
        return lax.rem(half + dy, 2)

    def ahead(dz):
        return lax.rem(z + dz, deep)

    def member(plane_at, z_at, core_at):
        return {"member": 2 * (plane_at * deep + z_at) + core_at, "domain": d}

    def other(core_step):
        return lax.rem(core + core_step, 2)

    def slot_place(s):
        k = s // 2
        dz = deep // 2 + (1 - 2 * lax.rem(k, 2)) * ((k + 1) // 2)
        return plane(1 - lax.rem(s, 2)), ahead(dz)

    def place_to(s):
        plane_at, z_at = slot_place(s)
        return plane_at * deep + z_at

    def peer(s):
        return {"member": 2 * place_to(s) + core, "domain": d}

    def crossing(q):
        return {
            "member": 2 * p + lax.rem(core + lax.rem(q, 2), 2),
            "domain": lax.rem(d + q // 2, count_d),
        }

    def around(dm, dd):
        return {
            "member": lax.rem(m + dm + count_m, count_m),
            "domain": lax.rem(d + dd + count_d, count_d),
        }

    def remote(src, dst, send, recv, device):
        return pltpu.make_async_remote_copy(
            src_ref=src, dst_ref=dst, send_sem=send, recv_sem=recv, device_id=device, device_id_type=MESH
        )

    loads = [
        pltpu.make_async_copy(source, target, local_sems.at[i])
        for i, (source, target) in enumerate(
            (
                (column_hbm, obs_int),
                (innovation_hbm, obs_real.at[0]),
                (weight_hbm, obs_real.at[1]),
                (sea_hbm, land_sea),
                (courant_hbm, fields.at[0:2, 0:32, :]),
                (depth_hbm, depth_row),
                (label_hbm, label_scalars),
                (label_hbm, label_vector),
                (pert_hbm, pert.at[pl.ds(0, 4)]),
            )
        )
    ]
    for copy in loads:
        copy.start()

    barrier = pltpu.get_barrier_semaphore()

    def greet_member(j, carry):
        device = {"member": lax.rem(m + j, count_m), "domain": d}
        pl.semaphore_signal(barrier, inc=1, device_id=device, device_id_type=MESH)
        return carry

    def greet_crossing(q, carry):
        pl.semaphore_signal(barrier, inc=1, device_id=crossing(q), device_id_type=MESH)
        return carry

    for dm, dd in AROUND:
        pl.semaphore_signal(barrier, inc=1, device_id=around(dm, dd), device_id_type=MESH)
    lax.fori_loop(1, count_m, greet_member, 0)
    lax.fori_loop(1, 2 * count_d, greet_crossing, 0)

    lane = lax.broadcasted_iota(jnp.int32, (32, 128), 1)
    for copy in loads[:5]:
        copy.wait()
    sea = land_sea[...].astype(F32)
    fields[2, 0:32, :] = sea
    turn[...] = jnp.zeros((2, 128, 128), F32)
    for t in range(NSTEP):
        turn[0, 16 * t : 16 * t + 16, 0:32] = (obs_int[t] - d * 128).astype(F32)
        turn[0, 48 + 16 * t : 64 + 16 * t, 0:32] = obs_real[1, t]
        turn[1, 16 * t : 16 * t + 16, 0:32] = -obs_real[1, t] * obs_real[0, t]
    across = turn[0].T[0:32, :]
    push = turn[1].T[0:32, :]
    column = across.astype(jnp.int32)
    pick[...] = column
    for t in range(NSTEP):
        w_sum = jnp.zeros((32, 128), F32)
        g_sum = jnp.zeros((32, 128), F32)
        for j in range(16 * t, 16 * t + 16):
            hit = column[:, j : j + 1] == lane
            w_sum = w_sum + jnp.where(hit, across[:, 48 + j : 49 + j], 0.0)
            g_sum = g_sum + jnp.where(hit, push[:, j : j + 1], 0.0)
        fields[3 + t, 0:32, :] = w_sum
        fields[6 + t, 0:32, :] = g_sum
    first = jnp.zeros((32, 128), F32)
    last = jnp.zeros((32, 128), F32)
    for f in range(FIELDS):
        here = (lane >= EDGE * f) & (lane < EDGE * (f + 1))
        value = fields[f, 0:32, :]
        turned = value if f == 0 else pltpu.roll(value, EDGE * f, 1)
        first = jnp.where(here, turned, first)
        last = jnp.where(here, pltpu.roll(value, EDGE * (f + 1), 1), last)
    pack_out[0] = first
    pack_out[1] = last

    pl.semaphore_wait(barrier, 8 + (count_m - 1) + (2 * count_d - 1))

    def rows_of(dm):
        if dm == 0:
            return slice(0, 32), slice(0, 32)
        if dm == 1:
            return slice(24, 32), slice(40, 48)
        return slice(0, 8), slice(32, 40)

    def rim_copy(n, i):
        dm, dd = AROUND[i]
        src, dst = rows_of(dm)
        sem = 0
        if n == 0:
            if dd == 0:
                a, b = fields.at[:, src, :], fields.at[:, dst, :]
            else:
                side, sem = (0 if dd < 0 else 1), 1
                a, b = pack_out.at[side, src, :], pack_in.at[side, dst, :]
        else:
            at = 0 if dd == 0 else (48 if dd < 0 else 96)
            a = tile.at[n - 1, src, :]
            b = tile.at[n - 1, slice(dst.start + at, dst.stop + at), :]
        return remote(a, b, rim_send.at[n, sem], rim_recv.at[n, sem], around(dm, dd))

    def rim_wait(n):
        def both(ref, sem):
            copy = remote(ref, ref, rim_send.at[n, sem], rim_recv.at[n, sem], sibling)
            copy.wait_recv()
            copy.wait_send()

        if n == 0:
            both(fields.at[:, 32:48, :], 0)
            both(pack_in, 1)
        else:
            both(tile.at[n - 1, 32:144, :], 0)

    for i in range(8):
        rim_copy(0, i).start()
    share = remote(pert_hbm, pert.at[pl.ds(4, 4)], pert_sems.at[0], pert_sems.at[1], sibling)
    share.start()

    for copy in loads[5:8]:
        copy.wait()

    row_i = lax.broadcasted_iota(jnp.int32, (128, 128), 0)
    lane_i = lax.broadcasted_iota(jnp.int32, (128, 128), 1)
    for t in range(tiles):
        gap = jnp.abs(lane_i + 128 * t - row_i)
        gap = jnp.minimum(gap, total - gap).astype(F32)
        x = 2.0 - 4.0 * gap / total
        value = (jnp.exp(x) + jnp.exp(-x)) / (2.0 * math.cosh(2.0))
        base[:, 128 * t : 128 * (t + 1)] = value
        base[:, total + 128 * t : total + 128 * (t + 1)] = value
        row = jnp.broadcast_to(depth_row[t : t + 1, :], (128, 128))
        turned = row.T
        depth_col[0, 128 * t : 128 * (t + 1), :] = turned
        depth_col[1, 128 * t : 128 * (t + 1), :] = 1.0 / turned
    blocks = total // LOC_ROWS
    spot = lax.broadcasted_iota(jnp.int32, (blocks, total), 1) // LOC_ROWS
    own_block = lax.broadcasted_iota(jnp.int32, (blocks, total), 0)
    labels = jnp.dot(
        jnp.broadcast_to(label_vector[...].astype(F32), (8, blocks)),
        (spot == own_block).astype(F32),
        preferred_element_type=F32,
    )[0:1, :]
    depth = jnp.concatenate([depth_row[t : t + 1, :] for t in range(tiles)], axis=1)
    depth_inv = 1.0 / depth

    def localize(s, carry):
        q = place_to(s)
        for h in range(2):
            label = label_scalars[0, 4 * q + 2 * core + h].astype(F32)
            factor = jnp.where(jnp.abs(labels - label) < 0.5, 2.0, 1.0)
            by = depth * factor
            by_inv = depth_inv * factor
            rows = pl.ds(pl.multiple_of(64 * q + 32 * core + 16 * h, 16), 16)
            base_rows = pl.ds(pl.multiple_of(64 * lax.rem(q, 2) + 32 * core + 16 * h, 16), 16)
            a = depth_col[0, rows, :]
            a_inv = depth_col[1, rows, :]
            out_rows = pl.ds(pl.multiple_of(32 * s + 16 * h, 16), 16)
            for t in range(tiles):
                cols = slice(128 * t, 128 * (t + 1))
                ratio = jnp.minimum(a * by_inv[:, cols], a_inv * by[:, cols])
                offset = pl.multiple_of(128 * (tiles - q // 2 + t), 128)
                loc[out_rows, cols] = (ratio * base[base_rows, pl.ds(offset, 128)]).astype(BF16)
        return carry

    split = peers // 2
    lax.fori_loop(0, split, localize, 0)

    rim_wait(0)

    lane48 = lax.broadcasted_iota(jnp.int32, (48, 128), 1)
    ext = []
    for f in range(FIELDS):
        right = pack_in[0] if f == 0 else pltpu.roll(pack_in[0], 128 - EDGE * f, 1)
        left = pltpu.roll(pack_in[1], 128 - EDGE * (f + 1), 1)
        ext.append(jnp.concatenate([fields[f], jnp.where(lane48 < 64, right, left)], axis=1))
    cu, cv, sea_ext = ext[0], ext[1], ext[2]
    coef[0] = 1.0 - jnp.abs(cu) - jnp.abs(cv)
    coef[1] = jnp.maximum(cu, 0.0)
    coef[2] = jnp.maximum(-cu, 0.0)
    coef[3] = jnp.maximum(cv, 0.0)
    coef[4] = jnp.maximum(-cv, 0.0)
    coef[5] = sea_ext
    for t in range(NSTEP):
        weight_ext[t] = ext[3 + t]
        force_ext[t] = ext[6 + t]

    def shift(value, by, axis):
        return pltpu.roll(value, by % value.shape[axis], axis)

    def advance(s):
        moved = coef[0] * s + coef[1] * shift(s, 1, 1) + coef[2] * shift(s, -1, 1)
        moved = moved + coef[3] * shift(s, 1, 0) + coef[4] * shift(s, -1, 0)
        return coef[5] * moved

    def retreat(adj):
        masked = coef[5] * adj
        back = coef[0] * masked + shift(coef[1] * masked, -1, 1) + shift(coef[2] * masked, 1, 1)
        return back + shift(coef[3] * masked, -1, 0) + shift(coef[4] * masked, 1, 0)

    def adjoint(forces):
        adj = retreat(forces[2])
        adj = retreat(adj + forces[1])
        return retreat(adj + forces[0])[0:32, 0:128]

    def slot(dy, dc, dz):
        return (2 * dy + dc) * deep + dz

    combos = [(0, 1), (1, 0), (1, 1)]
    near_steps = sorted((k for k in range(deep) if not low <= k < high), key=lambda k: -min(k, deep - k))
    far_count, near_count = high - low, 4 * len(near_steps) - 1

    def gathered(n, start, count, send_sem, recv_sem):
        ref = whole.at[n, pl.ds(start, count)]
        return remote(ref, ref, send_sem, recv_sem, sibling)

    def scatter_gather(n, meanwhile):
        whole[n, 0] = (sea * grad[n]).astype(BF16)

        def send(dy, dc, dz, sem):
            remote(
                whole.at[n, 0],
                whole.at[n, slot(dy, dc, dz)],
                gat_send.at[n, 0],
                gat_recv.at[n, sem],
                member(plane(dy), ahead(dz), other(dc)),
            ).start()

        for g, (start, stop) in enumerate(groups):
            for dz in range(start, stop):
                send(0, 0, dz, g)
        for dz in near_steps:
            for dy, dc in combos + [(0, 0)]:
                if (dy, dc, dz) != (0, 0, 0):
                    send(dy, dc, dz, 3)
        meanwhile()

        def weigh(dy, dc, start, stop):
            def body(dz, carry):
                q = plane(dy) * deep + ahead(deep - dz)
                rows = pl.ds(pl.multiple_of(64 * q + 32 * other(dc), 32), 32)
                v = whole[n, slot(dy, dc, dz)]
                for k in range(8):
                    weighted[rows, 128 * k : 128 * (k + 1)] = pert[k, rows, :] * v
                return carry

            lax.fori_loop(start, stop, body, 0)

        for g, (start, stop) in enumerate(groups):
            count = stop - start
            gathered(n, start, count, gat_send.at[n, 0], gat_recv.at[n, g]).wait_recv()
            for i, (dy, dc) in enumerate(combos):
                remote(
                    whole.at[n, pl.ds(start, count)],
                    whole.at[n, pl.ds(slot(dy, dc, start), count)],
                    gat_send.at[n, 1],
                    fwd_recv.at[n, 3 * g + i],
                    member(plane(dy), z, other(dc)),
                ).start()
        if far_count:
            weigh(0, 0, low, high)
        gathered(n, 0, near_count, gat_send.at[n, 0], gat_recv.at[n, 3]).wait_recv()
        for dy, dc in combos + [(0, 0)]:
            weigh(dy, dc, 0, low)
            if near:
                weigh(dy, dc, high, deep)
        for g, (start, stop) in enumerate(groups):
            for i, (dy, dc) in enumerate(combos):
                gathered(
                    n, slot(dy, dc, start), stop - start, gat_send.at[n, 1], fwd_recv.at[n, 3 * g + i]
                ).wait_recv()
                weigh(dy, dc, start, stop)

        def reduce_copy(s):
            return remote(rs_send.at[n, s], rs_recv.at[n, s], red_send.at[n], red_recv.at[n], peer(s))

        chunks = CHUNKS if peers % CHUNKS == 0 else 2
        slots = peers // chunks

        def share_of(s, i):
            rows = pl.ds(pl.multiple_of(64 * place_to(s) + 32 * core, 32), 32)
            rows_in = pl.ds(pl.multiple_of(32 * i, 32), 32)
            acc = pert[0, rows, :].astype(F32) * spread[rows_in, 0:128]
            for k in range(1, 8):
                acc = acc + pert[k, rows, :].astype(F32) * spread[rows_in, 128 * k : 128 * (k + 1)]
            return acc

        def chunk(ci, carry):
            first_row = pl.multiple_of(ci * slots * 32, 32)
            spread[...] = jnp.dot(
                loc[pl.ds(first_row, slots * 32), :], weighted[...], preferred_element_type=F32
            )

            def out(i, inner):
                s = ci * slots + i

                @pl.when(s < peers - 1)
                def _():
                    rs_send[n, s] = share_of(s, i).astype(BF16)
                    reduce_copy(s).start()

                return inner

            lax.fori_loop(0, slots, out, 0)
            return carry

        lax.fori_loop(0, chunks, chunk, 0)
        acc = share_of(peers - 1, slots - 1)
        remote(rs_send.at[n], rs_recv.at[n], red_send.at[n], red_recv.at[n], sibling).wait_recv()

        def collect(s, acc):
            return acc + rs_recv[n, s].astype(F32)

        acc = lax.fori_loop(0, peers - 1, collect, acc, unroll=True)
        tile[n, 0:32, :] = sea * acc / (ensemble - 1)
        for i in range(8):
            rim_copy(n + 1, i).start()

    def finish_sends(n):
        remote(rs_send.at[n], rs_recv.at[n], red_send.at[n], red_recv.at[n], sibling).wait_send()
        gathered(n, 0, far_count + near_count, gat_send.at[n, 0], gat_recv.at[n, 3]).wait_send()
        if far_count:
            gathered(n, 0, 3 * far_count, gat_send.at[n, 1], gat_recv.at[n, 3]).wait_send()

    def widened(n):
        rim_wait(n + 1)
        side = jnp.where(lane48 < 64, tile[n, 48:96, :], tile[n, 96:144, :])
        return jnp.concatenate([tile[n, 0:48, :], side], axis=1)

    def tangent(s):
        states = []
        for t in range(NSTEP):
            s = advance(s)
            states.append(s)
        return states

    def sample(states, n):
        got = jnp.zeros((32, 128), F32)
        for t in range(NSTEP):
            taken = jnp.take_along_axis(states[t][0:32, 0:128], pick[...], axis=1)
            got = jnp.where((lane >= 16 * t) & (lane < 16 * t + 16), taken, got)
        seen[n] = got

    def added(value):
        return jnp.sum(jnp.sum(value, axis=0, keepdims=True), axis=1, keepdims=True)

    def inner(x):
        return x[0:32, 0:128]

    grad[0] = adjoint([force_ext[t] for t in range(NSTEP)])

    def rest_of_setup():
        lax.fori_loop(split, peers, localize, 0)
        loads[8].wait()
        share.wait()

    scatter_gather(0, rest_of_setup)
    first_states = tangent(widened(0))
    pulls = [weight_ext[t] * first_states[t] for t in range(NSTEP)]
    grad[1] = adjoint(pulls) * SCALE
    results = []

    def rest_of_first():
        for t in range(NSTEP):
            force_ext[t] = pulls[t]
        sample(first_states, 0)
        results.append(added(sum(inner(pulls[t]) * inner(first_states[t]) for t in range(NSTEP))))

    scatter_gather(1, rest_of_first)
    misfit_11 = results[0]
    finish_sends(0)
    d1 = tile[0, 0:32, :]
    d2 = tile[1, 0:32, :]
    curve_11 = added(grad[0] * d1)
    curve_12 = added(grad[0] * d2 + grad[1] * d1)
    curve_22 = added(grad[1] * d2)
    second_states = tangent(widened(1))
    misfit_12 = added(sum(inner(force_ext[t]) * inner(second_states[t]) for t in range(NSTEP)))
    misfit_22 = added(
        sum(inner(weight_ext[t]) * inner(second_states[t]) * inner(second_states[t]) for t in range(NSTEP))
    )

    lane1 = lax.broadcasted_iota(jnp.int32, (1, 128), 1)
    sums = jnp.zeros((1, 128), F32)
    for i, value in enumerate((curve_11, curve_12, curve_22, misfit_11, misfit_12, misfit_22)):
        sums = jnp.where(lane1 == i, value, sums)

    def ar_refs(stage):
        return ar_a if stage == 0 else ar_b

    def ar_copy(stage, s):
        device = peer(s) if stage == 0 else crossing(s + 1)
        return remote(
            ar_send.at[stage], ar_refs(stage).at[s], ar_send_sem.at[stage], ar_recv_sem.at[stage], device
        )

    def ar_all(stage):
        ref = ar_refs(stage)
        return remote(ref, ref, ar_send_sem.at[stage], ar_recv_sem.at[stage], sibling)

    for stage, slots in ((0, peers - 1), (1, 2 * count_d - 1)):
        ar_send[stage] = sums

        def start(s, carry):
            ar_copy(stage, s).start()
            return carry

        lax.fori_loop(0, slots, start, 0)
        if stage == 0:
            sample(second_states, 1)
            finish_sends(1)
        ar_all(stage).wait_recv()
        sums = sums + jnp.sum(ar_refs(stage)[...], axis=0)

    def total_of(i):
        return jnp.sum(jnp.where(lane1 == i, sums, 0.0), axis=1, keepdims=True)

    curve_11, curve_12, curve_22 = total_of(0), total_of(1), total_of(2)
    misfit_11, misfit_12, misfit_22 = total_of(3), total_of(4), total_of(5)
    step_1 = curve_11 / (curve_11 + misfit_11)
    keep = 1.0 - step_1
    mix = step_1 * (1.0 / SCALE)
    curve = keep * keep * curve_11 - mix * keep * curve_12 + mix * mix * curve_22
    misfit = keep * keep * misfit_11 - 2.0 * mix * keep * misfit_12 + mix * mix * misfit_22
    step_2 = curve / (curve + misfit)
    a = -step_1 - step_2 * keep
    b = step_2 * mix
    increment_out[...] = a * d1 + b * d2
    turn[0, 0:32, :] = a * seen[0] + b * seen[1]
    down = turn[0].T
    for t in range(NSTEP):
        equivalents_out[t] = down[16 * t : 16 * t + 16, 0:32]
    ar_all(0).wait_send()
    ar_all(1).wait_send()


def per_device(
    perturb, courant, land_sea, basin_labels, row_depth, sample_column, innovation, error_weight
):
    members, total, width = perturb.shape
    rows = land_sea.shape[0]
    count_m = lax.axis_size("member")
    count_d = lax.axis_size("domain")
    peers = count_m // 2
    chunks = CHUNKS if peers % CHUNKS == 0 else 2
    vmem = pl.BlockSpec(memory_space=pltpu.VMEM)
    hbm = pl.BlockSpec(memory_space=pltpu.HBM)
    slots = innovation.shape[2]
    dma = pltpu.SemaphoreType.DMA
    increment, equivalents = pl.pallas_call(
        functools.partial(kernel, members * count_m),
        out_shape=(
            jax.ShapeDtypeStruct((rows, width), F32),
            jax.ShapeDtypeStruct((NSTEP, slots, rows), F32),
        ),
        in_specs=[hbm] * 8,
        out_specs=(vmem, vmem),
        scratch_shapes=[
            pltpu.VMEM((2 * members, total, width), BF16),
            pltpu.VMEM((total // 2, total), BF16),
            pltpu.VMEM((total, 2 * members * width), BF16),
            pltpu.VMEM((total // 2 // chunks, 2 * members * width), F32),
            pltpu.VMEM((128, 2 * total), F32),
            pltpu.VMEM((2, total, 128), F32),
            pltpu.VMEM((total // 128, 128), F32),
            pltpu.SMEM((1, basin_labels.shape[0]), jnp.int32),
            pltpu.VMEM((1, basin_labels.shape[0]), jnp.int32),
            pltpu.VMEM((rows, width), jnp.int32),
            pltpu.VMEM((NSTEP, slots, rows), jnp.int32),
            pltpu.VMEM((2, NSTEP, slots, rows), F32),
            pltpu.VMEM((2, 128, 128), F32),
            pltpu.VMEM((FIELDS, 48, 128), F32),
            pltpu.VMEM((2, 32, 128), F32),
            pltpu.VMEM((2, 48, 128), F32),
            pltpu.VMEM((6, 48, 256), F32),
            pltpu.VMEM((NSTEP, 48, 256), F32),
            pltpu.VMEM((NSTEP, 48, 256), F32),
            pltpu.VMEM((2, count_m, 32, 128), BF16),
            pltpu.VMEM((2, peers - 1, 32, 128), BF16),
            pltpu.VMEM((2, peers - 1, 32, 128), BF16),
            pltpu.VMEM((2, 32, 128), F32),
            pltpu.VMEM((2, 144, 128), F32),
            pltpu.VMEM((2, 32, 128), F32),
            pltpu.VMEM((32, 128), jnp.int32),
            pltpu.VMEM((2, 1, 128), F32),
            pltpu.VMEM((peers - 1, 1, 128), F32),
            pltpu.VMEM((2 * count_d - 1, 1, 128), F32),
            dma((9,)),
            dma((2,)),
            dma((3, 2)),
            dma((3, 2)),
            dma((2, 2)),
            dma((2, 4)),
            dma((2, 9)),
            dma((2,)),
            dma((2,)),
            dma((2,)),
            dma((2,)),
        ],
        compiler_params=pltpu.CompilerParams(
            collective_id=0, has_side_effects=True, vmem_limit_bytes=60 * 1024 * 1024
        ),
    )(
        perturb,
        courant,
        land_sea,
        basin_labels.reshape(1, -1),
        row_depth.reshape(-1, 128),
        jnp.transpose(sample_column, (0, 2, 1)),
        jnp.transpose(innovation, (0, 2, 1)),
        jnp.transpose(error_weight, (0, 2, 1)),
    )
    return increment, jnp.transpose(equivalents, (0, 2, 1))


def solution(mesh):
    in_specs = (
        P("member", None, "domain"),
        P(None, "member", "domain"),
        P("member", "domain"),
        P(),
        P(),
        P(None, "member", "domain"),
        P(None, "member", "domain"),
        P(None, "member", "domain"),
    )
    out_specs = (P("member", "domain"), P(None, "member", "domain"))
    return jax.shard_map(
        per_device, mesh=mesh, in_specs=in_specs, out_specs=out_specs, check_vma=False
    )
```

```python
import functools
import math

import jax
import jax.numpy as jnp
from jax import lax
from jax.experimental import pallas as pl
from jax.experimental.pallas import tpu as pltpu
from jax.sharding import PartitionSpec as P

NSTEP = 3
LOC_ROWS = 16
FIELDS = 9
CHUNKS = 4
EDGE = 8
SCALE = 2.0**-10
MESH = pl.DeviceIdType.MESH
F32 = jnp.float32
BF16 = jnp.bfloat16
AROUND = [(1, 1), (1, -1), (-1, 1), (-1, -1), (0, 1), (0, -1), (1, 0), (-1, 0)]


def kernel(
    ensemble,
    pert_hbm,
    courant_hbm,
    sea_hbm,
    label_hbm,
    depth_hbm,
    column_hbm,
    innovation_hbm,
    weight_hbm,
    increment_out,
    equivalents_out,
    pert,
    loc,
    weighted,
    spread,
    base,
    depth_col,
    depth_row,
    label_scalars,
    label_vector,
    land_sea,
    obs_int,
    obs_real,
    turn,
    fields,
    pack_out,
    pack_in,
    coef,
    weight_ext,
    force_ext,
    whole,
    rs_send,
    rs_recv,
    grad,
    tile,
    seen,
    pick,
    ar_send,
    ar_a,
    ar_b,
    local_sems,
    pert_sems,
    rim_send,
    rim_recv,
    gat_send,
    gat_recv,
    fwd_recv,
    red_send,
    red_recv,
    ar_send_sem,
    ar_recv_sem,
):
    count_m = lax.axis_size("member")
    count_d = lax.axis_size("domain")
    m = lax.axis_index("member")
    d = lax.axis_index("domain")
    peers = count_m // 2
    deep = peers // 2
    total = 32 * count_m
    tiles = total // 128
    core = lax.rem(m, 2)
    p = m // 2
    half = p // deep
    z = lax.rem(p, deep)
    sibling = {"member": 2 * p + 1 - core, "domain": d}

    near = min(2, deep // 6)
    low, high = max(near, 1), deep - near
    third = (high - low) // 3
    groups = [(low + third, high - third), (low, low + third), (high - third, high)]
    groups = [group for group in groups if group[0] < group[1]]

    def plane(dy):
        return lax.rem(half + dy, 2)

    def ahead(dz):
        return lax.rem(z + dz, deep)

    def member(plane_at, z_at, core_at):
        return {"member": 2 * (plane_at * deep + z_at) + core_at, "domain": d}

    def other(core_step):
        return lax.rem(core + core_step, 2)

    def slot_place(s):
        k = s // 2
        dz = deep // 2 + (1 - 2 * lax.rem(k, 2)) * ((k + 1) // 2)
        return plane(1 - lax.rem(s, 2)), ahead(dz)

    def place_to(s):
        plane_at, z_at = slot_place(s)
        return plane_at * deep + z_at

    def peer(s):
        return {"member": 2 * place_to(s) + core, "domain": d}

    def crossing(q):
        return {
            "member": 2 * p + lax.rem(core + lax.rem(q, 2), 2),
            "domain": lax.rem(d + q // 2, count_d),
        }

    def around(dm, dd):
        return {
            "member": lax.rem(m + dm + count_m, count_m),
            "domain": lax.rem(d + dd + count_d, count_d),
        }

    def remote(src, dst, send, recv, device):
        return pltpu.make_async_remote_copy(
            src_ref=src, dst_ref=dst, send_sem=send, recv_sem=recv, device_id=device, device_id_type=MESH
        )

    loads = [
        pltpu.make_async_copy(source, target, local_sems.at[i])
        for i, (source, target) in enumerate(
            (
                (column_hbm, obs_int),
                (innovation_hbm, obs_real.at[0]),
                (weight_hbm, obs_real.at[1]),
                (sea_hbm, land_sea),
                (courant_hbm, fields.at[0:2, 0:32, :]),
                (depth_hbm, depth_row),
                (label_hbm, label_scalars),
                (label_hbm, label_vector),
                (pert_hbm, pert.at[pl.ds(0, 4)]),
            )
        )
    ]
    for copy in loads:
        copy.start()

    barrier = pltpu.get_barrier_semaphore()

    def greet_member(j, carry):
        device = {"member": lax.rem(m + j, count_m), "domain": d}
        pl.semaphore_signal(barrier, inc=1, device_id=device, device_id_type=MESH)
        return carry

    def greet_crossing(q, carry):
        pl.semaphore_signal(barrier, inc=1, device_id=crossing(q), device_id_type=MESH)
        return carry

    for dm, dd in AROUND:
        pl.semaphore_signal(barrier, inc=1, device_id=around(dm, dd), device_id_type=MESH)
    lax.fori_loop(1, count_m, greet_member, 0)
    lax.fori_loop(1, 2 * count_d, greet_crossing, 0)

    lane = lax.broadcasted_iota(jnp.int32, (32, 128), 1)
    for copy in loads[:5]:
        copy.wait()
    sea = land_sea[...].astype(F32)
    fields[2, 0:32, :] = sea
    turn[...] = jnp.zeros((2, 128, 128), F32)
    for t in range(NSTEP):
        turn[0, 16 * t : 16 * t + 16, 0:32] = (obs_int[t] - d * 128).astype(F32)
        turn[0, 48 + 16 * t : 64 + 16 * t, 0:32] = obs_real[1, t]
        turn[1, 16 * t : 16 * t + 16, 0:32] = -obs_real[1, t] * obs_real[0, t]
    across = turn[0].T[0:32, :]
    push = turn[1].T[0:32, :]
    column = across.astype(jnp.int32)
    pick[...] = column
    for t in range(NSTEP):
        w_sum = jnp.zeros((32, 128), F32)
        g_sum = jnp.zeros((32, 128), F32)
        for j in range(16 * t, 16 * t + 16):
            hit = column[:, j : j + 1] == lane
            w_sum = w_sum + jnp.where(hit, across[:, 48 + j : 49 + j], 0.0)
            g_sum = g_sum + jnp.where(hit, push[:, j : j + 1], 0.0)
        fields[3 + t, 0:32, :] = w_sum
        fields[6 + t, 0:32, :] = g_sum
    first = jnp.zeros((32, 128), F32)
    last = jnp.zeros((32, 128), F32)
    for f in range(FIELDS):
        here = (lane >= EDGE * f) & (lane < EDGE * (f + 1))
        value = fields[f, 0:32, :]
        turned = value if f == 0 else pltpu.roll(value, EDGE * f, 1)
        first = jnp.where(here, turned, first)
        last = jnp.where(here, pltpu.roll(value, EDGE * (f + 1), 1), last)
    pack_out[0] = first
    pack_out[1] = last

    pl.semaphore_wait(barrier, 8 + (count_m - 1) + (2 * count_d - 1))

    def rows_of(dm):
        if dm == 0:
            return slice(0, 32), slice(0, 32)
        if dm == 1:
            return slice(24, 32), slice(40, 48)
        return slice(0, 8), slice(32, 40)

    def rim_copy(n, i):
        dm, dd = AROUND[i]
        src, dst = rows_of(dm)
        sem = 0
        if n == 0:
            if dd == 0:
                a, b = fields.at[:, src, :], fields.at[:, dst, :]
            else:
                side, sem = (0 if dd < 0 else 1), 1
                a, b = pack_out.at[side, src, :], pack_in.at[side, dst, :]
        else:
            at = 0 if dd == 0 else (48 if dd < 0 else 96)
            a = tile.at[n - 1, src, :]
            b = tile.at[n - 1, slice(dst.start + at, dst.stop + at), :]
        return remote(a, b, rim_send.at[n, sem], rim_recv.at[n, sem], around(dm, dd))

    def rim_parts(n):
        if n == 0:
            return ((fields.at[:, 32:48, :], 0), (pack_in, 1))
        return ((tile.at[n - 1, 32:144, :], 0),)

    def rim_wait(n):
        for ref, sem in rim_parts(n):
            remote(ref, ref, rim_send.at[n, sem], rim_recv.at[n, sem], sibling).wait_recv()

    def rim_sent(n):
        for ref, sem in rim_parts(n):
            remote(ref, ref, rim_send.at[n, sem], rim_recv.at[n, sem], sibling).wait_send()

    for i in range(8):
        rim_copy(0, i).start()
    share = remote(pert_hbm, pert.at[pl.ds(4, 4)], pert_sems.at[0], pert_sems.at[1], sibling)
    share.start()

    for copy in loads[5:8]:
        copy.wait()

    row_i = lax.broadcasted_iota(jnp.int32, (128, 128), 0)
    lane_i = lax.broadcasted_iota(jnp.int32, (128, 128), 1)
    for t in range(tiles):
        gap = jnp.abs(lane_i + 128 * t - row_i)
        gap = jnp.minimum(gap, total - gap).astype(F32)
        x = 2.0 - 4.0 * gap / total
        value = (jnp.exp(x) + jnp.exp(-x)) / (2.0 * math.cosh(2.0))
        base[:, 128 * t : 128 * (t + 1)] = value
        base[:, total + 128 * t : total + 128 * (t + 1)] = value
        row = jnp.broadcast_to(depth_row[t : t + 1, :], (128, 128))
        turned = row.T
        depth_col[0, 128 * t : 128 * (t + 1), :] = turned
        depth_col[1, 128 * t : 128 * (t + 1), :] = 1.0 / turned
    blocks = total // LOC_ROWS
    spot = lax.broadcasted_iota(jnp.int32, (blocks, total), 1) // LOC_ROWS
    own_block = lax.broadcasted_iota(jnp.int32, (blocks, total), 0)
    labels = jnp.dot(
        jnp.broadcast_to(label_vector[...].astype(F32), (8, blocks)),
        (spot == own_block).astype(F32),
        preferred_element_type=F32,
    )[0:1, :]
    depth = jnp.concatenate([depth_row[t : t + 1, :] for t in range(tiles)], axis=1)
    depth_inv = 1.0 / depth

    def localize(s, carry):
        q = place_to(s)
        for h in range(2):
            label = label_scalars[0, 4 * q + 2 * core + h].astype(F32)
            factor = jnp.where(jnp.abs(labels - label) < 0.5, 2.0, 1.0)
            by = depth * factor
            by_inv = depth_inv * factor
            rows = pl.ds(pl.multiple_of(64 * q + 32 * core + 16 * h, 16), 16)
            base_rows = pl.ds(pl.multiple_of(64 * lax.rem(q, 2) + 32 * core + 16 * h, 16), 16)
            a = depth_col[0, rows, :]
            a_inv = depth_col[1, rows, :]
            out_rows = pl.ds(pl.multiple_of(32 * s + 16 * h, 16), 16)
            for t in range(tiles):
                cols = slice(128 * t, 128 * (t + 1))
                ratio = jnp.minimum(a * by_inv[:, cols], a_inv * by[:, cols])
                offset = pl.multiple_of(128 * (tiles - q // 2 + t), 128)
                loc[out_rows, cols] = (ratio * base[base_rows, pl.ds(offset, 128)]).astype(BF16)
        return carry

    split = peers // 2
    lax.fori_loop(0, split, localize, 0)

    rim_wait(0)

    lane48 = lax.broadcasted_iota(jnp.int32, (48, 128), 1)
    ext = []
    for f in range(FIELDS):
        right = pack_in[0] if f == 0 else pltpu.roll(pack_in[0], 128 - EDGE * f, 1)
        left = pltpu.roll(pack_in[1], 128 - EDGE * (f + 1), 1)
        ext.append(jnp.concatenate([fields[f], jnp.where(lane48 < 64, right, left)], axis=1))
    cu, cv, sea_ext = ext[0], ext[1], ext[2]
    coef[0] = 1.0 - jnp.abs(cu) - jnp.abs(cv)
    coef[1] = jnp.maximum(cu, 0.0)
    coef[2] = jnp.maximum(-cu, 0.0)
    coef[3] = jnp.maximum(cv, 0.0)
    coef[4] = jnp.maximum(-cv, 0.0)
    coef[5] = sea_ext
    for t in range(NSTEP):
        weight_ext[t] = ext[3 + t]
        force_ext[t] = ext[6 + t]

    def shift(value, by, axis):
        return pltpu.roll(value, by % value.shape[axis], axis)

    def advance(s):
        moved = coef[0] * s + coef[1] * shift(s, 1, 1) + coef[2] * shift(s, -1, 1)
        moved = moved + coef[3] * shift(s, 1, 0) + coef[4] * shift(s, -1, 0)
        return coef[5] * moved

    def retreat(adj):
        masked = coef[5] * adj
        back = coef[0] * masked + shift(coef[1] * masked, -1, 1) + shift(coef[2] * masked, 1, 1)
        return back + shift(coef[3] * masked, -1, 0) + shift(coef[4] * masked, 1, 0)

    def adjoint(forces):
        adj = retreat(forces[2])
        adj = retreat(adj + forces[1])
        return retreat(adj + forces[0])[0:32, 0:128]

    def slot(dy, dc, dz):
        return (2 * dy + dc) * deep + dz

    combos = [(0, 1), (1, 0), (1, 1)]
    near_steps = sorted((k for k in range(deep) if not low <= k < high), key=lambda k: -min(k, deep - k))
    far_count, near_count = high - low, 4 * len(near_steps) - 1

    def gathered(n, start, count, send_sem, recv_sem):
        ref = whole.at[n, pl.ds(start, count)]
        return remote(ref, ref, send_sem, recv_sem, sibling)

    def scatter_gather(n, meanwhile):
        whole[n, 0] = (sea * grad[n]).astype(BF16)

        def send(dy, dc, dz, sem):
            remote(
                whole.at[n, 0],
                whole.at[n, slot(dy, dc, dz)],
                gat_send.at[n, 0],
                gat_recv.at[n, sem],
                member(plane(dy), ahead(dz), other(dc)),
            ).start()

        for g, (start, stop) in enumerate(groups):
            for dz in range(start, stop):
                send(0, 0, dz, g)
        for dz in near_steps:
            for dy, dc in combos + [(0, 0)]:
                if (dy, dc, dz) != (0, 0, 0):
                    send(dy, dc, dz, 3)
        meanwhile()

        def weigh(dy, dc, start, stop):
            def body(dz, carry):
                q = plane(dy) * deep + ahead(deep - dz)
                rows = pl.ds(pl.multiple_of(64 * q + 32 * other(dc), 32), 32)
                v = whole[n, slot(dy, dc, dz)]
                for k in range(8):
                    weighted[rows, 128 * k : 128 * (k + 1)] = pert[k, rows, :] * v
                return carry

            lax.fori_loop(start, stop, body, 0)

        for g, (start, stop) in enumerate(groups):
            count = stop - start
            gathered(n, start, count, gat_send.at[n, 0], gat_recv.at[n, g]).wait_recv()
            for i, (dy, dc) in enumerate(combos):
                remote(
                    whole.at[n, pl.ds(start, count)],
                    whole.at[n, pl.ds(slot(dy, dc, start), count)],
                    gat_send.at[n, 1],
                    fwd_recv.at[n, 3 * g + i],
                    member(plane(dy), z, other(dc)),
                ).start()
        if far_count:
            weigh(0, 0, low, high)
        gathered(n, 0, near_count, gat_send.at[n, 0], gat_recv.at[n, 3]).wait_recv()
        for dy, dc in combos + [(0, 0)]:
            weigh(dy, dc, 0, low)
            if near:
                weigh(dy, dc, high, deep)
        for g, (start, stop) in enumerate(groups):
            for i, (dy, dc) in enumerate(combos):
                gathered(
                    n, slot(dy, dc, start), stop - start, gat_send.at[n, 1], fwd_recv.at[n, 3 * g + i]
                ).wait_recv()
                weigh(dy, dc, start, stop)

        def reduce_copy(s):
            return remote(rs_send.at[n, s], rs_recv.at[n, s], red_send.at[n], red_recv.at[n], peer(s))

        chunks = CHUNKS if peers % CHUNKS == 0 else 2
        slots = peers // chunks

        def share_of(s, i):
            rows = pl.ds(pl.multiple_of(64 * place_to(s) + 32 * core, 32), 32)
            rows_in = pl.ds(pl.multiple_of(32 * i, 32), 32)
            acc = pert[0, rows, :].astype(F32) * spread[rows_in, 0:128]
            for k in range(1, 8):
                acc = acc + pert[k, rows, :].astype(F32) * spread[rows_in, 128 * k : 128 * (k + 1)]
            return acc

        def chunk(ci, carry):
            first_row = pl.multiple_of(ci * slots * 32, 32)
            spread[...] = jnp.dot(
                loc[pl.ds(first_row, slots * 32), :], weighted[...], preferred_element_type=F32
            )

            def out(i, inner):
                s = ci * slots + i

                @pl.when(s < peers - 1)
                def _():
                    rs_send[n, s] = share_of(s, i).astype(BF16)
                    reduce_copy(s).start()

                return inner

            lax.fori_loop(0, slots, out, 0)
            return carry

        lax.fori_loop(0, chunks, chunk, 0)
        acc = share_of(peers - 1, slots - 1)
        remote(rs_send.at[n], rs_recv.at[n], red_send.at[n], red_recv.at[n], sibling).wait_recv()

        def collect(s, acc):
            return acc + rs_recv[n, s].astype(F32)

        acc = lax.fori_loop(0, peers - 1, collect, acc, unroll=True)
        tile[n, 0:32, :] = sea * acc / (ensemble - 1)
        for i in range(8):
            rim_copy(n + 1, i).start()

    def finish_sends(n):
        remote(rs_send.at[n], rs_recv.at[n], red_send.at[n], red_recv.at[n], sibling).wait_send()
        gathered(n, 0, far_count + near_count, gat_send.at[n, 0], gat_recv.at[n, 3]).wait_send()
        if far_count:
            gathered(n, 0, 3 * far_count, gat_send.at[n, 1], gat_recv.at[n, 3]).wait_send()

    def widened(n):
        rim_wait(n + 1)
        side = jnp.where(lane48 < 64, tile[n, 48:96, :], tile[n, 96:144, :])
        return jnp.concatenate([tile[n, 0:48, :], side], axis=1)

    def tangent(s):
        states = []
        for t in range(NSTEP):
            s = advance(s)
            states.append(s)
        return states

    def sample(states, n):
        got = jnp.zeros((32, 128), F32)
        for t in range(NSTEP):
            taken = jnp.take_along_axis(states[t][0:32, 0:128], pick[...], axis=1)
            got = jnp.where((lane >= 16 * t) & (lane < 16 * t + 16), taken, got)
        turn[n, 0:32, :] = got
        seen[n] = turn[n].T[0:48, 0:32]

    def added(value):
        return jnp.sum(jnp.sum(value, axis=0, keepdims=True), axis=1, keepdims=True)

    def inner(x):
        return x[0:32, 0:128]

    grad[0] = adjoint([force_ext[t] for t in range(NSTEP)])

    def rest_of_setup():
        lax.fori_loop(split, peers, localize, 0)
        loads[8].wait()
        share.wait_recv()

    scatter_gather(0, rest_of_setup)
    first_states = tangent(widened(0))
    pulls = [weight_ext[t] * first_states[t] for t in range(NSTEP)]
    grad[1] = adjoint(pulls) * SCALE
    results = []

    def rest_of_first():
        for t in range(NSTEP):
            force_ext[t] = pulls[t]
        sample(first_states, 0)
        results.append(added(sum(inner(pulls[t]) * inner(first_states[t]) for t in range(NSTEP))))

    scatter_gather(1, rest_of_first)
    misfit_11 = results[0]
    finish_sends(0)
    d1 = tile[0, 0:32, :]
    d2 = tile[1, 0:32, :]
    curve_11 = added(grad[0] * d1)
    curve_12 = added(grad[0] * d2 + grad[1] * d1)
    curve_22 = added(grad[1] * d2)
    second_states = tangent(widened(1))
    misfit_12 = added(sum(inner(force_ext[t]) * inner(second_states[t]) for t in range(NSTEP)))
    misfit_22 = added(
        sum(inner(weight_ext[t]) * inner(second_states[t]) * inner(second_states[t]) for t in range(NSTEP))
    )

    lane1 = lax.broadcasted_iota(jnp.int32, (1, 128), 1)
    sums = jnp.zeros((1, 128), F32)
    for i, value in enumerate((curve_11, curve_12, curve_22, misfit_11, misfit_12, misfit_22)):
        sums = jnp.where(lane1 == i, value, sums)

    def ar_refs(stage):
        return ar_a if stage == 0 else ar_b

    def ar_copy(stage, s):
        device = peer(s) if stage == 0 else crossing(s + 1)
        return remote(
            ar_send.at[stage], ar_refs(stage).at[s], ar_send_sem.at[stage], ar_recv_sem.at[stage], device
        )

    def ar_all(stage):
        ref = ar_refs(stage)
        return remote(ref, ref, ar_send_sem.at[stage], ar_recv_sem.at[stage], sibling)

    for stage, slots in ((0, peers - 1), (1, 2 * count_d - 1)):
        ar_send[stage] = sums

        def start(s, carry):
            ar_copy(stage, s).start()
            return carry

        lax.fori_loop(0, slots, start, 0, unroll=True)
        if stage == 0:
            sample(second_states, 1)
            finish_sends(1)
            for n in range(3):
                rim_sent(n)
        ar_all(stage).wait_recv()
        sums = sums + jnp.sum(ar_refs(stage)[...], axis=0)

    def total_of(i):
        return jnp.sum(jnp.where(lane1 == i, sums, 0.0), axis=1, keepdims=True)

    curve_11, curve_12, curve_22 = total_of(0), total_of(1), total_of(2)
    misfit_11, misfit_12, misfit_22 = total_of(3), total_of(4), total_of(5)
    step_1 = curve_11 / (curve_11 + misfit_11)
    keep = 1.0 - step_1
    mix = step_1 * (1.0 / SCALE)
    curve = keep * keep * curve_11 - mix * keep * curve_12 + mix * mix * curve_22
    misfit = keep * keep * misfit_11 - 2.0 * mix * keep * misfit_12 + mix * mix * misfit_22
    step_2 = curve / (curve + misfit)
    a = -step_1 - step_2 * keep
    b = step_2 * mix
    increment_out[...] = a * d1 + b * d2
    for t in range(NSTEP):
        own = slice(16 * t, 16 * t + 16)
        equivalents_out[t] = a * seen[0, own, :] + b * seen[1, own, :]
    share.wait_send()
    ar_all(0).wait_send()
    ar_all(1).wait_send()


def settle(increment, equivalents, increment_out, equivalents_out):
    increment_out[...] = increment[...]
    equivalents_out[...] = equivalents[...]


def per_device(
    perturb, courant, land_sea, basin_labels, row_depth, sample_column, innovation, error_weight
):
    members, total, width = perturb.shape
    rows = land_sea.shape[0]
    count_m = lax.axis_size("member")
    count_d = lax.axis_size("domain")
    peers = count_m // 2
    chunks = CHUNKS if peers % CHUNKS == 0 else 2
    vmem = pl.BlockSpec(memory_space=pltpu.VMEM)
    hbm = pl.BlockSpec(memory_space=pltpu.HBM)
    slots = innovation.shape[2]
    dma = pltpu.SemaphoreType.DMA
    shapes = (
        jax.ShapeDtypeStruct((rows, width), F32),
        jax.ShapeDtypeStruct((NSTEP, slots, rows), F32),
    )
    results = pl.pallas_call(
        functools.partial(kernel, members * count_m),
        out_shape=shapes,
        in_specs=[hbm] * 8,
        out_specs=(vmem, vmem),
        scratch_shapes=[
            pltpu.VMEM((2 * members, total, width), BF16),
            pltpu.VMEM((total // 2, total), BF16),
            pltpu.VMEM((total, 2 * members * width), BF16),
            pltpu.VMEM((total // 2 // chunks, 2 * members * width), F32),
            pltpu.VMEM((128, 2 * total), F32),
            pltpu.VMEM((2, total, 128), F32),
            pltpu.VMEM((total // 128, 128), F32),
            pltpu.SMEM((1, basin_labels.shape[0]), jnp.int32),
            pltpu.VMEM((1, basin_labels.shape[0]), jnp.int32),
            pltpu.VMEM((rows, width), jnp.int32),
            pltpu.VMEM((NSTEP, slots, rows), jnp.int32),
            pltpu.VMEM((2, NSTEP, slots, rows), F32),
            pltpu.VMEM((2, 128, 128), F32),
            pltpu.VMEM((FIELDS, 48, 128), F32),
            pltpu.VMEM((2, 32, 128), F32),
            pltpu.VMEM((2, 48, 128), F32),
            pltpu.VMEM((6, 48, 256), F32),
            pltpu.VMEM((NSTEP, 48, 256), F32),
            pltpu.VMEM((NSTEP, 48, 256), F32),
            pltpu.VMEM((2, count_m, 32, 128), BF16),
            pltpu.VMEM((2, peers - 1, 32, 128), BF16),
            pltpu.VMEM((2, peers - 1, 32, 128), BF16),
            pltpu.VMEM((2, 32, 128), F32),
            pltpu.VMEM((2, 144, 128), F32),
            pltpu.VMEM((2, NSTEP * slots, rows), F32),
            pltpu.VMEM((32, 128), jnp.int32),
            pltpu.VMEM((2, 1, 128), F32),
            pltpu.VMEM((peers - 1, 1, 128), F32),
            pltpu.VMEM((2 * count_d - 1, 1, 128), F32),
            dma((9,)),
            dma((2,)),
            dma((3, 2)),
            dma((3, 2)),
            dma((2, 2)),
            dma((2, 4)),
            dma((2, 9)),
            dma((2,)),
            dma((2,)),
            dma((2,)),
            dma((2,)),
        ],
        compiler_params=pltpu.CompilerParams(
            collective_id=0, has_side_effects=True, vmem_limit_bytes=60 * 1024 * 1024
        ),
    )(
        perturb,
        courant,
        land_sea,
        basin_labels.reshape(1, -1),
        row_depth.reshape(-1, 128),
        jnp.transpose(sample_column, (0, 2, 1)),
        jnp.transpose(innovation, (0, 2, 1)),
        jnp.transpose(error_weight, (0, 2, 1)),
    )
    increment, equivalents = pl.pallas_call(
        settle,
        out_shape=shapes,
        in_specs=[vmem, vmem],
        out_specs=(vmem, vmem),
        compiler_params=pltpu.CompilerParams(vmem_limit_bytes=60 * 1024 * 1024),
    )(*results)
    return increment, jnp.transpose(equivalents, (0, 2, 1))


def solution(mesh):
    in_specs = (
        P("member", None, "domain"),
        P(None, "member", "domain"),
        P("member", "domain"),
        P(),
        P(),
        P(None, "member", "domain"),
        P(None, "member", "domain"),
        P(None, "member", "domain"),
    )
    out_specs = (P("member", "domain"), P(None, "member", "domain"))
    return jax.shard_map(
        per_device, mesh=mesh, in_specs=in_specs, out_specs=out_specs, check_vma=False
    )
```
